128 devices in a mesh: cat: 4 (over z), row: 2 (over x_hi), loop: 16 (over x_lo, y, core).
Axes of the slice: x: 4 (x_hi: 2, x_lo: 2; x = x_hi * 2 + x_lo), y: 4, z: 4, core: 2. Of those that a mesh axis runs over, the one named last changes fastest.
Arguments:
- queries: bfloat16 [65536, 512], P(('cat', 'row', 'loop')), may hold values from -60 to 60
- categories: int32 [65536, 1], P(('cat', 'row', 'loop')), may hold values from 0 to 3; in each aligned block of 512 rows (0 to 511, 512 to 1023, ...) at most 256 rows name the same one
- item_keys: bfloat16 [32768, 512], P(('cat', 'row', 'loop')), may hold values from -40 to 40
- item_values: bfloat16 [32768, 512], P(('cat', 'row', 'loop')), may hold values from -6 to 6
Outputs:
- soft_targets: bfloat16 [65536, 512], P(('cat', 'row', 'loop'))
The draws below stay inside these ranges and needn't reach their ends.
Inputs may be any that keep to these rules, and one draw needn't show every extreme that they name: `categories`: in the 512 rows of one device no category appears more than 256 times.
All inputs are finite; a program needn't handle non-finite values.
Results may differ from the reference program's by a relative error of at most 0.024.
Values may be sent and summed in bfloat16 or wider, within the bound.
No kernel may reach another device: no remote copies, remote signals or barrier semaphores. Data moves between devices by JAX's collectives and lax.ppermute only.
A program may use at most 128 MiB of HBM per device.

```python
import math
import jax
import jax.numpy as jnp
import numpy as np
from jax import lax

D = 512
R_DEV = 512
CAP = 256
CATS = 4
ITEMS = 8192
REQUESTS = 65536


def draw_queries(key, part):
    key = jax.random.fold_in(key, 11)
    base = jnp.clip(jax.random.normal(jax.random.fold_in(key, 1), (REQUESTS, D), jnp.float32), -6.0, 6.0)
    return base.astype(jnp.bfloat16)


def draw_item_keys(key, part):
    key = jax.random.fold_in(key, 13)
    base = jnp.clip(jax.random.normal(jax.random.fold_in(key, 1), (CATS * ITEMS, D), jnp.float32), -6.0, 6.0)
    return base.astype(jnp.bfloat16)


def block_scale(rng, dims, shards, least, top_value):
    def one(axis_at, blocks):
        steps = jax.random.uniform(jax.random.fold_in(jax.random.fold_in(rng, 6), axis_at), (blocks,), jnp.float32, least / len(shards), top_value / len(shards))
        return jnp.repeat(jnp.exp(steps), dims[axis_at] // blocks).reshape((-1,) + (1,) * (len(dims) - axis_at - 1))

    factor_of = one(*shards[0])
    for cut in shards[1:]:
        factor_of = factor_of * one(*cut)
    return factor_of


def routed_block(own_key, own, number, rows, number_of, top, most, skew):
    ranking = jax.random.permutation(own_key, number_of)
    crowded, ordinary = shares(number_of, rows * top, most, skew, True), shares(number_of, rows * top, most, skew, False)
    places = jnp.arange(number_of)

    def named(sizes, turn):
        used = int((sizes > 0).sum())
        fixed = max(1, used // 4)
        moved = fixed + (places - fixed + turn * (used - fixed)) % max(1, number_of - fixed)
        return jnp.zeros((number_of,), jnp.int32).at[ranking[jnp.where(places < fixed, places, moved)]].set(jnp.asarray(sizes, jnp.int32))

    sizes = jnp.where(number % 4 == 0, named(crowded, number // 4), named(ordinary, number - number // 4 - 1))
    mixed = jax.random.permutation(jax.random.fold_in(own, 3), number_of)
    giver, taker = mixed[0:number_of // 2 * 2:2], mixed[1:number_of // 2 * 2:2]
    room = jnp.minimum(sizes[giver] - 1, most - sizes[taker]) // 2
    room = jnp.where((giver == ranking[0]) | (taker == ranking[0]) | (sizes[taker] == 0), 0, jnp.maximum(room, 0))
    moved = jax.random.randint(jax.random.fold_in(own, 4), (number_of // 2,), 0, 1 << 20) % (room + 1)
    sizes = sizes.at[giver].add(-moved).at[taker].add(moved)
    members = jnp.searchsorted(jnp.cumsum(sizes), jnp.arange(rows * top), side="right").astype(jnp.int32)
    table = members.reshape(top, rows).T
    table = table[jax.random.permutation(jax.random.fold_in(own, 1), rows)]
    turn = jax.random.randint(jax.random.fold_in(own, 2), (rows, 1), 0, top)
    return jnp.take_along_axis(table, (jnp.arange(top)[None, :] + turn) % top, axis=1)


def shares(count, total, reach, slope, full):
    weights = [(1 << 20) // math.isqrt(rank ** slope) + 1 for rank in range(1, count + 1)]
    largest = reach if full else min(reach, max(-(-total // count), total * weights[0] // sum(weights)))
    least = 1 if total - largest >= count - 1 else 0
    counts, spare = [largest] + [least] * (count - 1), total - largest - least * (count - 1)
    while spare > 0:
        movable = [i for i in range(1, count) if counts[i] < largest] or [i for i in range(1, count) if counts[i] < reach]
        pool, budget = sum([weights[i] for i in movable]), spare
        for i in movable:
            addition = min(reach - counts[i], max(1, budget * weights[i] // pool), spare)
            counts[i] = counts[i] + addition
            spare = spare - addition
    return np.array(counts)


def normal_values(rng, extent, scale, most, cuts=(), kind=jnp.bfloat16):
    result = jax.random.normal(rng, extent, jnp.float32) * scale
    if len(cuts) > 0:
        result = block_scale(rng, extent, cuts, -0.22, 0.18) * result
    return jnp.clip(result, min=-most, max=most).astype(kind)


def setup_inputs(seed: int = 0) -> dict:
    key_list = jax.random.split(jax.random.key(seed), 5)
    queries = draw_queries(jax.random.fold_in(key_list[4], 71), 0)
    categories_keys = jax.random.split(jax.random.fold_in(key_list[1], 1), REQUESTS // R_DEV)
    categories_turns = jax.random.permutation(jax.random.fold_in(key_list[1], 3), REQUESTS // R_DEV)
    categories = jax.vmap(lambda own, number: routed_block(jax.random.fold_in(key_list[1], 2), own, number, R_DEV, CATS, 1, CAP, 2))(categories_keys, categories_turns).reshape((REQUESTS, 1))
    item_keys = draw_item_keys(jax.random.fold_in(key_list[4], 71), 0)
    item_values = normal_values(key_list[3], (CATS * ITEMS, D), 1.0, 6.0, ((0, 128),))
    return dict(queries=queries, categories=categories, item_keys=item_keys, item_values=item_values)


def category_targets(block_query, key_rows, value_rows):
    score_scale = 1.4 / math.sqrt(D)
    scores = lax.dot_general(block_query, key_rows, (((1,), (1,)), ((), ())), preferred_element_type=jnp.float32) * score_scale
    row_max = lax.optimization_barrier(jnp.max(scores, axis=1))
    expo = jnp.exp(scores - row_max[:, None])
    totals = lax.optimization_barrier(jnp.sum(expo, axis=1))
    weighted = jnp.dot(expo.astype(jnp.bfloat16), value_rows, preferred_element_type=jnp.float32)
    pooled = weighted / totals[:, None]
    return pooled * lax.rsqrt(lax.optimization_barrier(jnp.mean(pooled * pooled, axis=1, keepdims=True)) + 1e-06)

def reference(queries, categories, item_keys, item_values):
    cat_ids = categories[:, 0].astype(jnp.int32)
    sort_order = jnp.argsort(cat_ids, stable=True).astype(jnp.int32)
    sorted_query = queries[sort_order]
    sorted_cats = cat_ids[sort_order]
    block_count = REQUESTS // R_DEV
    query_blocks = sorted_query.reshape(block_count, R_DEV, D)
    cat_blocks = sorted_cats.reshape(block_count, R_DEV)

    def one_block(block_args):
        block_query, block_cats = block_args
        first_cat = block_cats[0]
        last_cat = block_cats[-1]

        def per_category(results, cat_index):

            def compute(operand):
                key_rows = lax.dynamic_slice_in_dim(item_keys, (cat_index * ITEMS).astype(jnp.int32), ITEMS, 0)
                value_rows = lax.dynamic_slice_in_dim(item_values, (cat_index * ITEMS).astype(jnp.int32), ITEMS, 0)
                return category_targets(block_query, key_rows, value_rows)

            def skipped(operand):
                return jnp.zeros((R_DEV, D), jnp.float32)
            normed = lax.cond((cat_index >= first_cat) & (cat_index <= last_cat), compute, skipped, 0)
            results = jnp.where((block_cats == cat_index)[:, None], normed, results)
            return (results, 0)
        results, unused = lax.scan(per_category, jnp.zeros((R_DEV, D), jnp.float32), jnp.arange(CATS, dtype=jnp.int32))
        return results
    blocked = lax.map(one_block, (query_blocks, cat_blocks))
    flat = blocked.reshape(REQUESTS, D)
    placed = jnp.zeros((REQUESTS, D), jnp.float32).at[sort_order].set(flat)
    return placed.astype(jnp.bfloat16)
```

```python
import functools
import math

import jax
import jax.numpy as jnp
from jax import lax
from jax.experimental import pallas as pl
from jax.experimental.pallas import tpu as pltpu
from jax.sharding import PartitionSpec as P

D = 512
CAP = 256
CATS = 4
SCALE = 1.4 / math.sqrt(D) * math.log2(math.e)
BF = jnp.bfloat16
F32 = jnp.float32
PLANE = ("row", "loop")
VMEM = pl.BlockSpec(memory_space=pltpu.VMEM)


def place(x, y, core):
    return ((x % 4) * 4 + y % 4) * 2 + core


def hops(first, step):
    pairs = []
    for x in range(4):
        for y in range(4):
            for core in range(2):
                along_x = (core == 0) == first
                to = place(x + step, y, core) if along_x else place(x, y + step, core)
                pairs.append((place(x, y, core), to))
    return pairs


def first_hop(a, step):
    return lax.ppermute(a, PLANE, hops(True, step))


def second_hop(a, step):
    return lax.ppermute(a, PLANE, hops(False, step))


def swap_cores(a):
    return lax.ppermute(a, PLANE, [(i, i ^ 1) for i in range(32)])


def shift_plane(a, step):
    return lax.ppermute(a, "cat", [(i, (i + step) % CATS) for i in range(CATS)])


def nt(a, b):
    return lax.dot_general(a, b, (((1,), (1,)), ((), ())), preferred_element_type=F32)


def nn(a, b):
    return jnp.dot(a, b, preferred_element_type=F32)


def params(mib):
    return pltpu.CompilerParams(vmem_limit_bytes=mib * 1024 * 1024)


def dispatch_kernel(cat_ref, q_ref, o0, o1, o2, o3, slot_ref):
    rows = cat_ref.shape[1]
    me = lax.axis_index("cat")
    rel = (cat_ref[...] - me + CATS) & 3
    named = lax.broadcasted_iota(jnp.int32, (16, rows), 0) == rel
    before = lax.broadcasted_iota(jnp.int32, (rows, rows), 0) < lax.broadcasted_iota(
        jnp.int32, (rows, rows), 1
    )
    rank = nn(named.astype(BF), before.astype(BF))
    rank = jnp.sum(jnp.where(named, rank, 0.0), axis=0, keepdims=True)
    slot = rel * CAP + rank.astype(jnp.int32)
    q = q_ref[...]
    for r, out in enumerate((o0, o1, o2, o3)):
        pick = lax.broadcasted_iota(jnp.int32, (CAP, rows), 0) + r * CAP == slot
        out[...] = nn(pick.astype(BF), q).astype(BF)
    column = jnp.transpose(jnp.broadcast_to(slot.astype(F32), (128, rows)))
    slot_ref[...] = column.astype(jnp.int32)


def dispatch(cats, queries):
    rows = queries.shape[0]
    return pl.pallas_call(
        dispatch_kernel,
        out_shape=[jax.ShapeDtypeStruct((CAP, D), BF)] * CATS
        + [jax.ShapeDtypeStruct((rows, 128), jnp.int32)],
        in_specs=[VMEM] * 2,
        out_specs=[VMEM] * 5,
        compiler_params=params(32),
    )(cats, queries)


def fold_tile(q, keys, values, m_old, l_old, acc_old):
    scores = [nt(q, k[...]) for k in keys]
    top = functools.reduce(jnp.maximum, scores)
    m_new = jnp.max(top, axis=1, keepdims=True)
    if m_old is not None:
        m_new = jnp.maximum(m_new, m_old)
    total = None
    out = None
    for s, v in zip(scores, values):
        e = jnp.exp2((s - m_new) * SCALE)
        t = jnp.sum(e, axis=1, keepdims=True)
        o = nn(e.astype(BF), v[...])
        total = t if total is None else total + t
        out = o if out is None else out + o
    if m_old is not None:
        back = jnp.exp2((m_old - m_new) * SCALE)
        total = total + l_old * back
        out = out + acc_old * back
    return m_new, total, out


def fold_kernel(tiles, blocks, begin, *refs):
    refs = list(refs)
    qs = [refs.pop(0) for _ in range(tiles)]
    keys = [refs.pop(0) for _ in range(blocks)]
    values = [refs.pop(0) for _ in range(blocks)]
    if not begin:
        acc_in, ml_in = refs.pop(0), refs.pop(0)
    acc, ml = refs
    for t in range(tiles):
        rows = pl.ds(t * CAP, CAP)
        old = (None, None, None)
        if not begin:
            old = (ml_in[rows, 0:1], ml_in[rows, 128:129], acc_in[rows, :])
        m, l, a = fold_tile(qs[t][...], keys, values, *old)
        acc[rows, :] = a
        ml[rows, 0:128] = jnp.broadcast_to(m, (CAP, 128))
        ml[rows, 128:256] = jnp.broadcast_to(l, (CAP, 128))


def fold(qs, blocks, state):
    tiles, n = len(qs), len(blocks)
    args = list(qs) + [b[0] for b in blocks] + [b[1] for b in blocks] + list(state or ())
    aliases = {} if state is None else {len(args) - 2: 0, len(args) - 1: 1}
    rows = tiles * CAP
    return pl.pallas_call(
        functools.partial(fold_kernel, tiles, n, state is None),
        out_shape=[
            jax.ShapeDtypeStruct((rows, D), F32),
            jax.ShapeDtypeStruct((rows, 256), F32),
        ],
        in_specs=[VMEM] * len(args),
        out_specs=[VMEM] * 2,
        input_output_aliases=aliases,
        compiler_params=params(48),
        cost_estimate=pl.CostEstimate(
            flops=4 * rows * n * 256 * D,
            bytes_accessed=n * 512 * D * 2 + rows * D * 10,
            transcendentals=rows * n * 256,
        ),
    )(*args)


def parts_of(x):
    high = x.astype(BF)
    rest = x - high.astype(F32)
    middle = rest.astype(BF)
    return high, middle, (rest - middle.astype(F32)).astype(BF)


def pack_kernel(acc, ml, out):
    m = ml[:, 0:128]
    l = ml[:, 128:256]
    out[:, 0:D] = (acc[...] / l[:, 0:1]).astype(BF)
    lane = lax.broadcasted_iota(jnp.int32, m.shape, 1)
    packed = jnp.zeros(m.shape, F32)
    for i, part in enumerate(parts_of(m) + parts_of(l)):
        packed = jnp.where(lane == i, part.astype(F32), packed)
    out[:, D : D + 128] = packed.astype(BF)


def pack(state, rows):
    half = [
        pl.BlockSpec((rows, D), lambda i: (1, 0)),
        pl.BlockSpec((rows, 256), lambda i: (1, 0)),
    ]
    return pl.pallas_call(
        pack_kernel,
        grid=(1,),
        out_shape=jax.ShapeDtypeStruct((rows, D + 128), BF),
        in_specs=half,
        out_specs=pl.BlockSpec((rows, D + 128), lambda i: (0, 0)),
        compiler_params=params(32),
    )(*state)


def finish_kernel(blocks, q, *refs):
    keys, values = refs[:blocks], refs[blocks : 2 * blocks]
    acc, ml, other, out = refs[2 * blocks :]
    packed = other[:, D : D + 128].astype(F32)
    m_own, l_own = ml[:, 0:1], ml[:, 128:129]
    m_far = packed[:, 0:1] + packed[:, 1:2] + packed[:, 2:3]
    l_far = packed[:, 3:4] + packed[:, 4:5] + packed[:, 5:6]
    m = jnp.maximum(m_own, m_far)
    w_own = jnp.exp2((m_own - m) * SCALE)
    w_far = jnp.exp2((m_far - m) * SCALE) * l_far
    merged = acc[...] * w_own + other[:, 0:D].astype(F32) * w_far
    total = l_own * w_own + w_far
    m, total, merged = fold_tile(q[...], keys, values, m, total, merged)
    pooled = merged / total
    mean = jnp.mean(pooled * pooled, axis=1, keepdims=True)
    out[...] = (pooled * lax.rsqrt(mean + 1e-06)).astype(BF)


def finish(q, blocks, state, other, tile):
    n = len(blocks)
    whole = pl.BlockSpec((CAP, D), lambda i: (0, 0))
    return pl.pallas_call(
        functools.partial(finish_kernel, n),
        grid=(1,),
        out_shape=jax.ShapeDtypeStruct((CAP, D), BF),
        in_specs=[whole] * (1 + 2 * n)
        + [
            pl.BlockSpec((CAP, D), lambda i: (tile, 0)),
            pl.BlockSpec((CAP, 256), lambda i: (tile, 0)),
            pl.BlockSpec((CAP, D + 128), lambda i: (tile, 0)),
        ],
        out_specs=whole,
        compiler_params=params(32),
    )(q, *[b[0] for b in blocks], *[b[1] for b in blocks], *state, other)


def collect_kernel(slot_ref, r0, r1, r2, r3, out):
    rows = slot_ref.shape[0]
    slot = jnp.concatenate([slot_ref[...]] * 2, axis=1)
    lane = lax.broadcasted_iota(jnp.int32, (rows, CAP), 1)
    total = None
    for r, ref in enumerate((r0, r1, r2, r3)):
        pick = (lane + r * CAP == slot).astype(BF)
        part = nn(pick, ref[...])
        total = part if total is None else total + part
    out[...] = total.astype(BF)


def collect(slots, returned):
    rows = slots.shape[0]
    return pl.pallas_call(
        collect_kernel,
        out_shape=jax.ShapeDtypeStruct((rows, D), BF),
        in_specs=[VMEM] * 5,
        out_specs=VMEM,
        compiler_params=params(32),
    )(slots, *returned)


def shards(queries, categories, item_keys, item_values):
    rows = queries.shape[0]
    *sent, slots = dispatch(categories.reshape(1, rows), queries)
    own = [sent[0]] + [shift_plane(sent[r], r) for r in (1, 2, 3)]
    qs = own + [swap_cores(q) for q in own]

    here = (item_keys, item_values)
    left = tuple(first_hop(a, 1) for a in here)
    right = tuple(first_hop(a, -1) for a in here)
    far = (first_hop(left[0], 1), first_hop(right[1], -1))
    near, across = [], []
    for block in (here, left, right, far):
        up = tuple(second_hop(a, 1) for a in block)
        down = tuple(second_hop(a, -1) for a in block)
        near.append([up, down])
        across.append((second_hop(up[0], 1), second_hop(down[1], -1)))

    state = fold(qs, [here, left, right, far], None)
    for i in range(3):
        state = fold(qs, near[i] + [across[i]], state)
    state = fold(qs, near[3], state)
    other = swap_cores(pack(state, CATS * CAP))
    last = [across[3], tuple(swap_cores(a) for a in across[3])]
    returned = [None] * CATS
    for r in (2, 1, 3, 0):
        done = finish(own[r], last, state, other, r)
        returned[r] = shift_plane(done, -r) if r else done
    return collect(slots, returned)


def solution(mesh):
    placed = P(("cat", "row", "loop"), None)
    return jax.shard_map(
        shards,
        mesh=mesh,
        in_specs=(placed,) * 4,
        out_specs=placed,
        check_vma=False,
    )
```

```python
import functools
import math

import jax
import jax.numpy as jnp
from jax import lax
from jax.experimental import pallas as pl
from jax.experimental.pallas import tpu as pltpu
from jax.sharding import PartitionSpec as P

D = 512
CAP = 256
CATS = 4
BLOCK = 256
SCALE = 1.4 / math.sqrt(D) * math.log2(math.e)
BF = jnp.bfloat16
F32 = jnp.float32
PLANE = ("row", "loop")
VMEM = pl.BlockSpec(memory_space=pltpu.VMEM)


def place(x, y, core):
    return ((x % 4) * 4 + y % 4) * 2 + core


def hops(first, step):
    pairs = []
    for x in range(4):
        for y in range(4):
            for core in range(2):
                along_x = (core == 0) == first
                to = place(x + step, y, core) if along_x else place(x, y + step, core)
                pairs.append((place(x, y, core), to))
    return pairs


def first_hop(a, step):
    return lax.ppermute(a, PLANE, hops(True, step))


def second_hop(a, step):
    return lax.ppermute(a, PLANE, hops(False, step))


def swap_cores(a):
    return lax.ppermute(a, PLANE, [(i, i ^ 1) for i in range(32)])


def plane_hop(a, step):
    pairs = []
    for cat in range(CATS):
        for i in range(32):
            to = (cat + (step if i % 2 == 0 else -step)) % CATS
            pairs.append((cat * 32 + i, to * 32 + i))
    return lax.ppermute(a, ("cat",) + PLANE, pairs)


def opposite_plane(a):
    return lax.ppermute(a, "cat", [(i, (i + 2) % CATS) for i in range(CATS)])


def after(a, *earlier):
    return lax.optimization_barrier((a, *earlier))[0]


def nt(a, b):
    return lax.dot_general(a, b, (((1,), (1,)), ((), ())), preferred_element_type=F32)


def nn(a, b):
    return jnp.dot(a, b, preferred_element_type=F32)


def params(mib):
    return pltpu.CompilerParams(vmem_limit_bytes=mib * 1024 * 1024)


def classes(cats):
    rows = cats.shape[1]
    ahead = cats - lax.axis_index("cat")
    rel = jnp.where(lax.axis_index("loop") % 2 == 0, ahead, -ahead) & (CATS - 1)
    named = lax.broadcasted_iota(jnp.int32, (16, rows), 0) == rel
    before = lax.broadcasted_iota(jnp.int32, (rows, rows), 0) < lax.broadcasted_iota(
        jnp.int32, (rows, rows), 1
    )
    rank = nn(named.astype(BF), before.astype(BF))
    rank = jnp.sum(jnp.where(named, rank, 0.0), axis=0, keepdims=True)
    return rel * CAP + rank.astype(jnp.int32)


def dispatch_kernel(cat_ref, far_cat_ref, q_ref, far_q_ref, out0, sent, far0, slot_ref):
    rows = cat_ref.shape[1]
    slot, far_slot = classes(cat_ref[...]), classes(far_cat_ref[...])
    iota = lax.broadcasted_iota(jnp.int32, (CAP, rows), 0)

    def pick(r, slots, ref):
        return nn((iota + r * CAP == slots).astype(BF), ref[...]).astype(BF)

    sent[0:CAP, :] = pick(1, slot, q_ref)
    sent[CAP : 2 * CAP, :] = pick(1, far_slot, far_q_ref)
    sent[2 * CAP : 3 * CAP, :] = pick(2, slot, q_ref)
    out0[...] = pick(0, slot, q_ref)
    far0[...] = pick(0, far_slot, far_q_ref)
    column = jnp.transpose(jnp.broadcast_to(slot.astype(F32), (128, rows)))
    slot_ref[...] = column.astype(jnp.int32)


def dispatch(cats, far_cats, queries, far_queries):
    rows = queries.shape[0]
    out = lambda n: jax.ShapeDtypeStruct((n, D), BF)
    return pl.pallas_call(
        dispatch_kernel,
        out_shape=[out(CAP), out(3 * CAP), out(CAP)]
        + [jax.ShapeDtypeStruct((rows, 128), jnp.int32)],
        in_specs=[VMEM] * 4,
        out_specs=[VMEM] * 4,
        compiler_params=params(16),
    )(cats, far_cats, queries, far_queries)


def softmax_tile(scores, values, old):
    m = jnp.max(functools.reduce(jnp.maximum, scores), axis=1, keepdims=True)
    if old is not None:
        m = jnp.maximum(m, old[0])
    es = [jnp.exp2((s - m) * SCALE) for s in scores]
    l = jnp.sum(functools.reduce(jnp.add, es), axis=1, keepdims=True)
    o = functools.reduce(jnp.add, [nn(e.astype(BF), v) for e, v in zip(es, values)])
    if old is not None:
        back = jnp.exp2((old[0] - m) * SCALE)
        l = l + old[1] * back
        o = o + old[2] * back
    return m, l, o


def parts_of(x):
    high = x.astype(BF)
    rest = x - high.astype(F32)
    middle = rest.astype(BF)
    return high, middle, (rest - middle.astype(F32)).astype(BF)


def two_lanes(m, l):
    lane = lax.broadcasted_iota(jnp.int32, (m.shape[0], 128), 1)
    return jnp.where(lane == 0, m, l)


def fold_kernel(plan, tiles, groups, inputs, packed, *refs):
    n_items, n_qs, has_state = inputs
    items, qs, rest = refs[:n_items], refs[n_items : n_items + n_qs], list(refs[n_items + n_qs :])
    states = []
    if has_state:
        states = [(rest.pop(0), rest.pop(0)) for _ in range(groups)]
    outs = rest
    jobs = []
    for i, (blocks, begin) in enumerate(plan):
        if blocks:
            jobs.append((i // CATS, i % CATS, tiles[i], blocks, begin))

    def score(job):
        ref, row = job[2]
        q = qs[ref][pl.ds(row, CAP), :]
        return [nt(q, items[a][pl.ds(b, BLOCK), :]) for a, b, _, _ in job[3]]

    scores = score(jobs[0])
    for n, (group, t, _, blocks, begin) in enumerate(jobs):
        ahead = score(jobs[n + 1]) if n + 1 < len(jobs) else None
        values = [items[c][pl.ds(d, BLOCK), :] for _, _, c, d in blocks]
        rows = pl.ds(t * CAP, CAP)
        old = None
        if not begin:
            acc, ml = states[group]
            old = (ml[rows, 0:1], ml[rows, 1:2], acc[rows, :])
        m, l, o = softmax_tile(scores, values, old)
        if packed:
            (out,) = outs
            out[rows, 0:D] = (o * (1.0 / l)).astype(BF)
            lane = lax.broadcasted_iota(jnp.int32, (CAP, 128), 1)
            extra = jnp.zeros((CAP, 128), F32)
            for i, part in enumerate(parts_of(m) + parts_of(l)):
                extra = jnp.where(lane == i, part.astype(F32), extra)
            out[rows, D : D + 128] = extra.astype(BF)
        else:
            acc, ml = outs[2 * group : 2 * group + 2]
            acc[rows, :] = o
            ml[rows, :] = two_lanes(m, l)
        scores = ahead


def fold(qs, tiles, items, plan, states, packed=False, weight=1):
    groups = len(tiles) // CATS
    flat = [a for s in states or () for a in s]
    args = [*items, *qs, *flat]
    rows = CATS * CAP
    aliases = {}
    if packed:
        out_shape = [jax.ShapeDtypeStruct((rows, D + 128), BF)]
    else:
        out_shape = [
            jax.ShapeDtypeStruct((rows, D), F32),
            jax.ShapeDtypeStruct((rows, 128), F32),
        ] * groups
        aliases = {len(args) - len(flat) + i: i for i in range(len(flat))}
    work = int(sum(len(blocks) for blocks, _ in plan) * CAP * BLOCK * weight)
    kernel = functools.partial(
        fold_kernel, plan, tiles, groups, (len(items), len(qs), states is not None), packed
    )
    out = pl.pallas_call(
        kernel,
        out_shape=out_shape,
        in_specs=[VMEM] * len(args),
        out_specs=[VMEM] * len(out_shape),
        input_output_aliases=aliases,
        compiler_params=params(24),
        cost_estimate=pl.CostEstimate(
            flops=4 * work * D, bytes_accessed=len(items) * BLOCK * D, transcendentals=work
        ),
    )(*args)
    return out[0] if packed else [tuple(out[2 * g : 2 * g + 2]) for g in range(groups)]


def merge_kernel(acc, ml, other, acc_out, ml_out):
    for t in range(CATS):
        rows = pl.ds(t * CAP, CAP)
        extra = other[rows, D : D + 128].astype(F32)
        m_own, l_own = ml[rows, 0:1], ml[rows, 1:2]
        m_far = extra[:, 0:1] + extra[:, 1:2] + extra[:, 2:3]
        l_far = extra[:, 3:4] + extra[:, 4:5] + extra[:, 5:6]
        m = jnp.maximum(m_own, m_far)
        w_own = jnp.exp2((m_own - m) * SCALE)
        w_far = jnp.exp2((m_far - m) * SCALE) * l_far
        acc_out[rows, :] = acc[rows, :] * w_own + other[rows, 0:D].astype(F32) * w_far
        ml_out[rows, :] = two_lanes(m, l_own * w_own + w_far)


def merge(state, other):
    return pl.pallas_call(
        merge_kernel,
        out_shape=[jax.ShapeDtypeStruct(a.shape, a.dtype) for a in state],
        in_specs=[VMEM] * 3,
        out_specs=[VMEM] * 2,
        input_output_aliases={0: 0, 1: 1},
        compiler_params=params(16),
    )(*state, other)


def finish_kernel(tiles, count, *refs):
    qs, stacks, (acc, ml, *outs) = refs[:4], refs[4 : 4 + count], refs[4 + count :]
    keys = [a[0:BLOCK, :] for a in stacks]
    values = [a[BLOCK : 2 * BLOCK, :] for a in stacks]

    def score(t):
        ref, row = tiles[t]
        q = qs[ref][pl.ds(row, CAP), :]
        return [nt(q, k) for k in keys]

    scores = score(0)
    for t in range(CATS):
        ahead = score(t + 1) if t + 1 < CATS else None
        rows = pl.ds(t * CAP, CAP)
        _, l, o = softmax_tile(scores, values, (ml[rows, 0:1], ml[rows, 1:2], acc[rows, :]))
        inverse = 1.0 / l
        mean = jnp.mean(o * o, axis=1, keepdims=True) * inverse * inverse
        outs[t][...] = (o * (inverse * lax.rsqrt(mean + 1e-06))).astype(BF)
        scores = ahead


def finish(qs, tiles, blocks, state):
    return pl.pallas_call(
        functools.partial(finish_kernel, tiles, len(blocks)),
        out_shape=[jax.ShapeDtypeStruct((CAP, D), BF)] * CATS,
        in_specs=[VMEM] * (6 + len(blocks)),
        out_specs=[VMEM] * CATS,
        compiler_params=params(16),
    )(*qs, *blocks, *state)


def collect_kernel(slot_ref, r0, r1, r2, r3, out):
    rows = slot_ref.shape[0]
    slot = jnp.concatenate([slot_ref[...]] * 2, axis=1)
    lane = lax.broadcasted_iota(jnp.int32, (rows, CAP), 1)
    total = None
    for r, ref in enumerate((r0, r1, r2, r3)):
        pick = (lane + r * CAP == slot).astype(BF)
        part = nn(pick, ref[0:CAP, :])
        total = part if total is None else total + part
    out[...] = total.astype(BF)


def collect(slots, returned):
    rows = slots.shape[0]
    return pl.pallas_call(
        collect_kernel,
        out_shape=jax.ShapeDtypeStruct((rows, D), BF),
        in_specs=[VMEM] * 5,
        out_specs=VMEM,
        compiler_params=params(16),
    )(slots, *returned)


def shards(queries, categories, item_keys, item_values):
    rows = queries.shape[0]
    cats = categories.reshape(1, rows)
    q0, sent, far_q0, slots = dispatch(cats, swap_cores(cats), queries, swap_cores(queries))
    here = jnp.concatenate([item_keys, item_values], axis=0)
    left, right = first_hop(here, 1), first_hop(here, -1)
    q12 = after(plane_hop(sent, 1), left, right)
    q2 = plane_hop(q12[2 * CAP :], 1)
    far_q12, far_q2 = swap_cores(q12), swap_cores(q2)
    early = [q0, q12, far_q0, far_q12]
    qs = early + [q2, far_q2]
    own = ((0, 0), (1, 0), (3, CAP), (4, 0))
    theirs = ((2, 0), (3, 0), (1, CAP), (5, 0))
    tiles = own + theirs

    pair = after(jnp.concatenate([left, right], axis=0), slots)
    up_pair, down_pair = second_hop(pair, 1), second_hop(pair, -1)
    far = first_hop(left, 1)
    whole = lambda i, j=0: (i, j, i, j + BLOCK)
    two = 2 * BLOCK

    def same(blocks):
        return ((tuple(blocks), False),) * (2 * CATS)

    first = tuple(whole(i) for i in range(3))
    plan = (((first, True),) * 3 + (((), True),)) * 2
    state = fold(early, tiles, [here, left, right], plan, None, weight=1)
    rest = jnp.concatenate([here, after(far, state[0][1])], axis=0)
    up_rest, down_rest = second_hop(rest, 1), second_hop(rest, -1)
    own_far = whole(3)
    plan = ((((own_far,), False),) * 3 + ((first + (own_far,), True),)) * 2
    state = fold(qs, tiles, [here, left, right, far], plan, state, weight=1)
    up_left = second_hop(after(up_pair[:two], state[0][1]), 1)
    down_right = second_hop(after(down_pair[two:], state[0][1]), -1)
    both = same([whole(i, j) for i in range(2) for j in (0, two)])
    state = fold(qs, tiles, [up_pair, down_pair], both, state, weight=1)
    up_here = second_hop(up_rest[:two], 1)
    down_far = second_hop(down_rest[two:], -1)
    mine, others = fold(qs, tiles, [up_rest, down_rest], both, state, weight=1)
    tail = [after(up_left, up_here, down_far), down_right]
    last_plan = same([whole(0), whole(1)])[:CATS]
    other = swap_cores(fold(qs, theirs, tail, last_plan, [others], True, weight=1))
    (mine,) = fold(qs, own, tail, last_plan, [mine], weight=1)
    merged = merge(mine, other)
    last = [up_here, down_far]
    last += [swap_cores(a) for a in last]
    mine_q = ((0, 0), (1, 0), (2, CAP), (3, 0))
    done = finish([q0, q12, far_q12, q2], mine_q, last, merged)
    back2 = opposite_plane(done[3])
    ahead, behind = plane_hop(done[1], -1), plane_hop(done[2], 1)
    return collect(slots, (done[0], ahead, back2, behind))


def solution(mesh):
    placed = P(("cat", "row", "loop"), None)
    return jax.shard_map(
        shards,
        mesh=mesh,
        in_specs=(placed,) * 4,
        out_specs=placed,
        check_vma=False,
    )
```

```python
import functools
import math

import jax
import jax.numpy as jnp
from jax import lax
from jax.experimental import pallas as pl
from jax.experimental.pallas import tpu as pltpu
from jax.sharding import PartitionSpec as P

D = 512
CAP = 256
CATS = 4
BLOCK = 256
SCALE = 1.4 / math.sqrt(D) * math.log2(math.e)
BF = jnp.bfloat16
F32 = jnp.float32
PLANE = ("row", "loop")
VMEM = pl.BlockSpec(memory_space=pltpu.VMEM)


def place(x, y, core):
    return ((x % 4) * 4 + y % 4) * 2 + core


def hops(first, step):
    pairs = []
    for x in range(4):
        for y in range(4):
            for core in range(2):
                along_x = (core == 0) == first
                to = place(x + step, y, core) if along_x else place(x, y + step, core)
                pairs.append((place(x, y, core), to))
    return pairs


def first_hop(a, step):
    return lax.ppermute(a, PLANE, hops(True, step))


def second_hop(a, step):
    return lax.ppermute(a, PLANE, hops(False, step))


def swap_cores(a):
    return lax.ppermute(a, PLANE, [(i, i ^ 1) for i in range(32)])


def plane_hop(a, step):
    pairs = []
    for cat in range(CATS):
        for i in range(32):
            to = (cat + (step if i % 2 == 0 else -step)) % CATS
            pairs.append((cat * 32 + i, to * 32 + i))
    return lax.ppermute(a, ("cat",) + PLANE, pairs)


def opposite_plane(a):
    return lax.ppermute(a, "cat", [(i, (i + 2) % CATS) for i in range(CATS)])


def after(a, *earlier):
    return lax.optimization_barrier((a, *earlier))[0]


def nt(a, b):
    return lax.dot_general(a, b, (((1,), (1,)), ((), ())), preferred_element_type=F32)


def nn(a, b):
    return jnp.dot(a, b, preferred_element_type=F32)


def params(mib):
    return pltpu.CompilerParams(vmem_limit_bytes=mib * 1024 * 1024)


def classes(cats):
    rows = cats.shape[1]
    ahead = cats - lax.axis_index("cat")
    rel = jnp.where(lax.axis_index("loop") % 2 == 0, ahead, -ahead) & (CATS - 1)
    named = lax.broadcasted_iota(jnp.int32, (16, rows), 0) == rel
    before = lax.broadcasted_iota(jnp.int32, (rows, rows), 0) < lax.broadcasted_iota(
        jnp.int32, (rows, rows), 1
    )
    rank = nn(named.astype(BF), before.astype(BF))
    rank = jnp.sum(jnp.where(named, rank, 0.0), axis=0, keepdims=True)
    return rel * CAP + rank.astype(jnp.int32)


def dispatch_kernel(cat_ref, far_cat_ref, q_ref, far_q_ref, out0, sent, far0, slot_ref):
    rows = cat_ref.shape[1]
    slot, far_slot = classes(cat_ref[...]), classes(far_cat_ref[...])
    iota = lax.broadcasted_iota(jnp.int32, (CAP, rows), 0)

    def pick(r, slots, ref):
        return nn((iota + r * CAP == slots).astype(BF), ref[...]).astype(BF)

    sent[0:CAP, :] = pick(1, slot, q_ref)
    sent[CAP : 2 * CAP, :] = pick(1, far_slot, far_q_ref)
    sent[2 * CAP : 3 * CAP, :] = pick(2, slot, q_ref)
    out0[...] = pick(0, slot, q_ref)
    far0[...] = pick(0, far_slot, far_q_ref)
    column = jnp.transpose(jnp.broadcast_to(slot.astype(F32), (128, rows)))
    slot_ref[...] = column.astype(jnp.int32)


def dispatch(cats, far_cats, queries, far_queries):
    rows = queries.shape[0]
    out = lambda n: jax.ShapeDtypeStruct((n, D), BF)
    return pl.pallas_call(
        dispatch_kernel,
        out_shape=[out(CAP), out(3 * CAP), out(CAP)]
        + [jax.ShapeDtypeStruct((rows, 128), jnp.int32)],
        in_specs=[VMEM] * 4,
        out_specs=[VMEM] * 4,
        compiler_params=params(16),
    )(cats, far_cats, queries, far_queries)


def softmax_tile(scores, values, old):
    m = jnp.max(functools.reduce(jnp.maximum, scores), axis=1, keepdims=True)
    if old is not None:
        m = jnp.maximum(m, old[0])
    es = [jnp.exp2((s - m) * SCALE) for s in scores]
    l = jnp.sum(functools.reduce(jnp.add, es), axis=1, keepdims=True)
    o = functools.reduce(jnp.add, [nn(e.astype(BF), v) for e, v in zip(es, values)])
    if old is not None:
        back = jnp.exp2((old[0] - m) * SCALE)
        l = l + old[1] * back
        o = o + old[2] * back
    return m, l, o


def parts_of(x):
    high = x.astype(BF)
    rest = x - high.astype(F32)
    middle = rest.astype(BF)
    return high, middle, (rest - middle.astype(F32)).astype(BF)


def two_lanes(m, l):
    lane = lax.broadcasted_iota(jnp.int32, (m.shape[0], 128), 1)
    return jnp.where(lane == 0, m, l)


def fold_kernel(plan, tiles, groups, inputs, packed, *refs):
    n_items, n_qs, has_state = inputs
    items, qs, rest = refs[:n_items], refs[n_items : n_items + n_qs], list(refs[n_items + n_qs :])
    states = []
    if has_state:
        states = [(rest.pop(0), rest.pop(0)) for _ in range(groups)]
    outs = rest
    jobs = []
    for i, (blocks, begin) in enumerate(plan):
        group, rows = i // CATS, pl.ds(i % CATS * CAP, CAP)
        if blocks:
            jobs.append((group, i % CATS, tiles[i], blocks, begin))
        elif not begin:
            for ref, out in zip(states[group], outs[2 * group : 2 * group + 2]):
                out[rows, :] = ref[rows, :]

    def score(job):
        ref, row = job[2]
        q = qs[ref][pl.ds(row, CAP), :]
        return [nt(q, items[a][pl.ds(b, BLOCK), :]) for a, b, _, _ in job[3]]

    scores = score(jobs[0])
    for n, (group, t, _, blocks, begin) in enumerate(jobs):
        ahead = score(jobs[n + 1]) if n + 1 < len(jobs) else None
        values = [items[c][pl.ds(d, BLOCK), :] for _, _, c, d in blocks]
        rows = pl.ds(t * CAP, CAP)
        old = None
        if not begin:
            acc, ml = states[group]
            old = (ml[rows, 0:1], ml[rows, 1:2], acc[rows, :])
        m, l, o = softmax_tile(scores, values, old)
        if packed:
            (out,) = outs
            out[rows, 0:D] = (o * (1.0 / l)).astype(BF)
            lane = lax.broadcasted_iota(jnp.int32, (CAP, 128), 1)
            extra = jnp.zeros((CAP, 128), F32)
            for i, part in enumerate(parts_of(m) + parts_of(l)):
                extra = jnp.where(lane == i, part.astype(F32), extra)
            out[rows, D : D + 128] = extra.astype(BF)
        else:
            acc, ml = outs[2 * group : 2 * group + 2]
            acc[rows, :] = o
            ml[rows, :] = two_lanes(m, l)
        scores = ahead


def fold(qs, tiles, items, plan, states, packed=False, weight=1):
    groups = len(tiles) // CATS
    flat = [a for s in states or () for a in s]
    args = [*items, *qs, *flat]
    rows = CATS * CAP
    aliases = {}
    if packed:
        out_shape = [jax.ShapeDtypeStruct((rows, D + 128), BF)]
    else:
        out_shape = [
            jax.ShapeDtypeStruct((rows, D), F32),
            jax.ShapeDtypeStruct((rows, 128), F32),
        ] * groups
        aliases = {len(args) - len(flat) + i: i for i in range(len(flat))}
    work = int(sum(len(blocks) for blocks, _ in plan) * CAP * BLOCK * weight)
    kernel = functools.partial(
        fold_kernel, plan, tiles, groups, (len(items), len(qs), states is not None), packed
    )
    out = pl.pallas_call(
        kernel,
        out_shape=out_shape,
        in_specs=[VMEM] * len(args),
        out_specs=[VMEM] * len(out_shape),
        input_output_aliases=aliases,
        compiler_params=params(24),
        cost_estimate=pl.CostEstimate(
            flops=4 * work * D, bytes_accessed=len(items) * BLOCK * D, transcendentals=work
        ),
    )(*args)
    return out[0] if packed else [tuple(out[2 * g : 2 * g + 2]) for g in range(groups)]


def merge_kernel(acc, ml, other, acc_out, ml_out):
    for t in range(CATS):
        rows = pl.ds(t * CAP, CAP)
        extra = other[rows, D : D + 128].astype(F32)
        m_own, l_own = ml[rows, 0:1], ml[rows, 1:2]
        m_far = extra[:, 0:1] + extra[:, 1:2] + extra[:, 2:3]
        l_far = extra[:, 3:4] + extra[:, 4:5] + extra[:, 5:6]
        m = jnp.maximum(m_own, m_far)
        w_own = jnp.exp2((m_own - m) * SCALE)
        w_far = jnp.exp2((m_far - m) * SCALE) * l_far
        acc_out[rows, :] = acc[rows, :] * w_own + other[rows, 0:D].astype(F32) * w_far
        ml_out[rows, :] = two_lanes(m, l_own * w_own + w_far)


def merge(state, other):
    return pl.pallas_call(
        merge_kernel,
        out_shape=[jax.ShapeDtypeStruct(a.shape, a.dtype) for a in state],
        in_specs=[VMEM] * 3,
        out_specs=[VMEM] * 2,
        input_output_aliases={0: 0, 1: 1},
        compiler_params=params(16),
    )(*state, other)


def finish_kernel(tiles, count, *refs):
    qs, stacks, (acc, ml, *outs) = refs[:4], refs[4 : 4 + count], refs[4 + count :]
    keys = [a[0:BLOCK, :] for a in stacks]
    values = [a[BLOCK : 2 * BLOCK, :] for a in stacks]

    def score(t):
        ref, row = tiles[t]
        q = qs[ref][pl.ds(row, CAP), :]
        return [nt(q, k) for k in keys]

    scores = score(0)
    for t in range(CATS):
        ahead = score(t + 1) if t + 1 < CATS else None
        rows = pl.ds(t * CAP, CAP)
        _, l, o = softmax_tile(scores, values, (ml[rows, 0:1], ml[rows, 1:2], acc[rows, :]))
        inverse = 1.0 / l
        mean = jnp.mean(o * o, axis=1, keepdims=True) * inverse * inverse
        outs[t][...] = (o * (inverse * lax.rsqrt(mean + 1e-06))).astype(BF)
        scores = ahead


def finish(qs, tiles, blocks, state):
    return pl.pallas_call(
        functools.partial(finish_kernel, tiles, len(blocks)),
        out_shape=[jax.ShapeDtypeStruct((CAP, D), BF)] * CATS,
        in_specs=[VMEM] * (6 + len(blocks)),
        out_specs=[VMEM] * CATS,
        compiler_params=params(16),
    )(*qs, *blocks, *state)


def collect_kernel(slot_ref, r0, r1, r2, r3, out):
    rows = slot_ref.shape[0]
    slot = jnp.concatenate([slot_ref[...]] * 2, axis=1)
    lane = lax.broadcasted_iota(jnp.int32, (rows, CAP), 1)
    total = None
    for r, ref in enumerate((r0, r1, r2, r3)):
        pick = (lane + r * CAP == slot).astype(BF)
        part = nn(pick, ref[0:CAP, :])
        total = part if total is None else total + part
    out[...] = total.astype(BF)


def collect(slots, returned):
    rows = slots.shape[0]
    return pl.pallas_call(
        collect_kernel,
        out_shape=jax.ShapeDtypeStruct((rows, D), BF),
        in_specs=[VMEM] * 5,
        out_specs=VMEM,
        compiler_params=params(16),
    )(slots, *returned)


def shards(queries, categories, item_keys, item_values):
    rows = queries.shape[0]
    cats = categories.reshape(1, rows)
    here = jnp.concatenate([item_keys, item_values], axis=0)
    far_cats = after(swap_cores(cats), here)
    q0, sent, far_q0, slots = dispatch(cats, far_cats, queries, swap_cores(queries))
    left, right = first_hop(here, 1), first_hop(here, -1)
    q12 = after(plane_hop(sent, 1), left, right)
    q2 = plane_hop(q12[2 * CAP :], 1)
    far_q12 = swap_cores(q12)
    far_q2 = swap_cores(after(q2, far_q12))
    early = [q0, q12, far_q0, far_q12]
    qs = early + [q2, far_q2]
    own = ((0, 0), (1, 0), (3, CAP), (4, 0))
    theirs = ((2, 0), (3, 0), (1, CAP), (5, 0))
    tiles = own + theirs

    pair = after(jnp.concatenate([left, right], axis=0), slots)
    up_pair, down_pair = second_hop(pair, 1), second_hop(pair, -1)
    far = first_hop(left, 1)
    whole = lambda i, j=0: (i, j, i, j + BLOCK)
    two = 2 * BLOCK

    def same(blocks):
        return ((tuple(blocks), False),) * (2 * CATS)

    first = tuple(whole(i) for i in range(3))
    plan = (((first, True),) * 3 + (((), True),)) * 2
    state = fold(early, tiles, [here, left, right], plan, None, weight=0.3)
    rest = jnp.concatenate([here, after(far, state[0][1])], axis=0)
    up_rest, down_rest = second_hop(rest, 1), second_hop(rest, -1)
    own_far = whole(3)
    plan = ((((own_far,), False),) * 3 + ((first + (own_far,), True),)) * 2
    state = fold(qs, tiles, [here, left, right, far], plan, state, weight=1)
    up_pair, down_pair = after(up_pair, state[0][1]), after(down_pair, state[0][1])
    up_left, down_right = second_hop(up_pair[:two], 1), second_hop(down_pair[two:], -1)
    both = same([whole(i, j) for i in range(2) for j in (0, two)])
    state = fold(qs, tiles, [up_pair, down_pair], both, state, weight=1)
    up_here = second_hop(up_rest[:two], 1)
    down_far = second_hop(down_rest[two:], -1)
    mine, others = state
    tail = [up_rest, down_rest, up_left, down_right]
    blocks = tuple([whole(i, j) for i in range(2) for j in (0, two)] + [whole(2), whole(3)])
    todo, skip = (blocks, False), ((), False)
    other = swap_cores(fold(qs, theirs, tail, (todo,) * 4, [others], True, weight=3))
    (mine,) = fold(qs, own, tail, (todo, todo, skip, skip), [mine], weight=3)
    tail = [after(up_rest, up_here, down_far), down_rest, up_left, down_right]
    (mine,) = fold(qs, own, tail, (skip, skip, todo, todo), [mine], weight=3)
    merged = merge(mine, other)
    last = [up_here, down_far]
    last += [swap_cores(a) for a in last]
    mine_q = ((0, 0), (1, 0), (2, CAP), (3, 0))
    done = finish([q0, q12, far_q12, q2], mine_q, last, merged)
    back2 = opposite_plane(done[3])
    ahead, behind = plane_hop(done[1], -1), plane_hop(done[2], 1)
    return collect(slots, (done[0], ahead, back2, behind))


def solution(mesh):
    placed = P(("cat", "row", "loop"), None)
    return jax.shard_map(
        shards,
        mesh=mesh,
        in_specs=(placed,) * 4,
        out_specs=placed,
        check_vma=False,
    )
```

```python
import functools
import math

import jax
import jax.numpy as jnp
from jax import lax
from jax.experimental import pallas as pl
from jax.experimental.pallas import tpu as pltpu
from jax.sharding import PartitionSpec as P

D = 512
CAP = 256
CATS = 4
BLOCK = 256
SCALE = 1.4 / math.sqrt(D) * math.log2(math.e)
BF = jnp.bfloat16
F32 = jnp.float32
PLANE = ("row", "loop")
VMEM = pl.BlockSpec(memory_space=pltpu.VMEM)


def place(x, y, core):
    return ((x % 4) * 4 + y % 4) * 2 + core


def hops(first, step):
    pairs = []
    for x in range(4):
        for y in range(4):
            for core in range(2):
                along_x = (core == 0) == first
                to = place(x + step, y, core) if along_x else place(x, y + step, core)
                pairs.append((place(x, y, core), to))
    return pairs


def first_hop(a, step):
    return lax.ppermute(a, PLANE, hops(True, step))


def second_hop(a, step):
    return lax.ppermute(a, PLANE, hops(False, step))


def swap_cores(a):
    return lax.ppermute(a, PLANE, [(i, i ^ 1) for i in range(32)])


def plane_hop(a, step):
    pairs = []
    for cat in range(CATS):
        for i in range(32):
            to = (cat + (step if i % 2 == 0 else -step)) % CATS
            pairs.append((cat * 32 + i, to * 32 + i))
    return lax.ppermute(a, ("cat",) + PLANE, pairs)


def opposite_plane(a):
    return lax.ppermute(a, "cat", [(i, (i + 2) % CATS) for i in range(CATS)])


def after(a, *earlier):
    return lax.optimization_barrier((a, *earlier))[0]


def nt(a, b):
    return lax.dot_general(a, b, (((1,), (1,)), ((), ())), preferred_element_type=F32)


def nn(a, b):
    return jnp.dot(a, b, preferred_element_type=F32)


def params(mib):
    return pltpu.CompilerParams(vmem_limit_bytes=mib * 1024 * 1024)


def classes(cats):
    rows = cats.shape[1]
    ahead = cats - lax.axis_index("cat")
    rel = jnp.where(lax.axis_index("loop") % 2 == 0, ahead, -ahead) & (CATS - 1)
    named = lax.broadcasted_iota(jnp.int32, (16, rows), 0) == rel
    before = lax.broadcasted_iota(jnp.int32, (rows, rows), 0) < lax.broadcasted_iota(
        jnp.int32, (rows, rows), 1
    )
    rank = nn(named.astype(BF), before.astype(BF))
    rank = jnp.sum(jnp.where(named, rank, 0.0), axis=0, keepdims=True)
    return rel * CAP + rank.astype(jnp.int32)


def dispatch_kernel(cat_ref, far_cat_ref, q_ref, far_q_ref, out0, out1, far1, out2, far0, slot_ref):
    rows = cat_ref.shape[1]
    slot, far_slot = classes(cat_ref[...]), classes(far_cat_ref[...])
    iota = lax.broadcasted_iota(jnp.int32, (CAP, rows), 0)

    def pick(r, slots, ref):
        return nn((iota + r * CAP == slots).astype(BF), ref[...]).astype(BF)

    out1[...] = pick(1, slot, q_ref)
    far1[...] = pick(1, far_slot, far_q_ref)
    out2[...] = pick(2, slot, q_ref)
    out0[...] = pick(0, slot, q_ref)
    far0[...] = pick(0, far_slot, far_q_ref)
    column = jnp.transpose(jnp.broadcast_to(slot.astype(F32), (128, rows)))
    slot_ref[...] = column.astype(jnp.int32)


def dispatch(cats, far_cats, queries, far_queries):
    rows = queries.shape[0]
    out = lambda n: jax.ShapeDtypeStruct((n, D), BF)
    return pl.pallas_call(
        dispatch_kernel,
        out_shape=[out(CAP)] * 5
        + [jax.ShapeDtypeStruct((rows, 128), jnp.int32)],
        in_specs=[VMEM] * 4,
        out_specs=[VMEM] * 6,
        compiler_params=params(16),
    )(cats, far_cats, queries, far_queries)


def softmax_tile(scores, values, old):
    m = jnp.max(functools.reduce(jnp.maximum, scores), axis=1, keepdims=True)
    if old is not None:
        m = jnp.maximum(m, old[0])
    es = [jnp.exp2((s - m) * SCALE) for s in scores]
    l = jnp.sum(functools.reduce(jnp.add, es), axis=1, keepdims=True)
    o = functools.reduce(jnp.add, [nn(e.astype(BF), v) for e, v in zip(es, values)])
    if old is not None:
        back = jnp.exp2((old[0] - m) * SCALE)
        l = l + old[1] * back
        o = o + old[2] * back
    return m, l, o


def parts_of(x):
    high = x.astype(BF)
    rest = x - high.astype(F32)
    middle = rest.astype(BF)
    return high, middle, (rest - middle.astype(F32)).astype(BF)


def two_lanes(m, l):
    lane = lax.broadcasted_iota(jnp.int32, (m.shape[0], 128), 1)
    return jnp.where(lane == 0, m, l)


def fold_kernel(plan, tiles, groups, inputs, packed, *refs):
    n_items, n_qs, has_state = inputs
    items, qs, rest = refs[:n_items], refs[n_items : n_items + n_qs], list(refs[n_items + n_qs :])
    states = []
    if has_state:
        states = [(rest.pop(0), rest.pop(0)) for _ in range(groups)]
    outs = rest
    jobs = []
    for i, (blocks, begin) in enumerate(plan):
        group, rows = i // CATS, pl.ds(i % CATS * CAP, CAP)
        if blocks:
            jobs.append((group, i % CATS, tiles[i], blocks, begin))
        elif not begin:
            for ref, out in zip(states[group], outs[2 * group : 2 * group + 2]):
                out[rows, :] = ref[rows, :]

    def score(job):
        ref, row = job[2]
        q = qs[ref][pl.ds(row, CAP), :]
        return [nt(q, items[a][pl.ds(b, BLOCK), :]) for a, b, _, _ in job[3]]

    scores = score(jobs[0])
    for n, (group, t, _, blocks, begin) in enumerate(jobs):
        ahead = score(jobs[n + 1]) if n + 1 < len(jobs) else None
        values = [items[c][pl.ds(d, BLOCK), :] for _, _, c, d in blocks]
        rows = pl.ds(t * CAP, CAP)
        old = None
        if not begin:
            acc, ml = states[group]
            old = (ml[rows, 0:1], ml[rows, 1:2], acc[rows, :])
        m, l, o = softmax_tile(scores, values, old)
        if packed:
            (out,) = outs
            out[rows, 0:D] = (o * (1.0 / l)).astype(BF)
            lane = lax.broadcasted_iota(jnp.int32, (CAP, 128), 1)
            extra = jnp.zeros((CAP, 128), F32)
            for i, part in enumerate(parts_of(m) + parts_of(l)):
                extra = jnp.where(lane == i, part.astype(F32), extra)
            out[rows, D : D + 128] = extra.astype(BF)
        else:
            acc, ml = outs[2 * group : 2 * group + 2]
            acc[rows, :] = o
            ml[rows, :] = two_lanes(m, l)
        scores = ahead


def fold(qs, tiles, items, plan, states, packed=False, weight=1):
    groups = len(tiles) // CATS
    flat = [a for s in states or () for a in s]
    args = [*items, *qs, *flat]
    rows = CATS * CAP
    aliases = {}
    if packed:
        out_shape = [jax.ShapeDtypeStruct((rows, D + 128), BF)]
    else:
        out_shape = [
            jax.ShapeDtypeStruct((rows, D), F32),
            jax.ShapeDtypeStruct((rows, 128), F32),
        ] * groups
        aliases = {len(args) - len(flat) + i: i for i in range(len(flat))}
    work = int(sum(len(blocks) for blocks, _ in plan) * CAP * BLOCK * weight)
    kernel = functools.partial(
        fold_kernel, plan, tiles, groups, (len(items), len(qs), states is not None), packed
    )
    out = pl.pallas_call(
        kernel,
        out_shape=out_shape,
        in_specs=[VMEM] * len(args),
        out_specs=[VMEM] * len(out_shape),
        input_output_aliases=aliases,
        compiler_params=params(24),
        cost_estimate=pl.CostEstimate(
            flops=4 * work * D, bytes_accessed=len(items) * BLOCK * D, transcendentals=work
        ),
    )(*args)
    return out[0] if packed else [tuple(out[2 * g : 2 * g + 2]) for g in range(groups)]


def merge_kernel(acc, ml, other, acc_out, ml_out):
    for t in range(CATS):
        rows = pl.ds(t * CAP, CAP)
        extra = other[rows, D : D + 128].astype(F32)
        m_own, l_own = ml[rows, 0:1], ml[rows, 1:2]
        m_far = extra[:, 0:1] + extra[:, 1:2] + extra[:, 2:3]
        l_far = extra[:, 3:4] + extra[:, 4:5] + extra[:, 5:6]
        m = jnp.maximum(m_own, m_far)
        w_own = jnp.exp2((m_own - m) * SCALE)
        w_far = jnp.exp2((m_far - m) * SCALE) * l_far
        acc_out[rows, :] = acc[rows, :] * w_own + other[rows, 0:D].astype(F32) * w_far
        ml_out[rows, :] = two_lanes(m, l_own * w_own + w_far)


def merge(state, other):
    return pl.pallas_call(
        merge_kernel,
        out_shape=[jax.ShapeDtypeStruct(a.shape, a.dtype) for a in state],
        in_specs=[VMEM] * 3,
        out_specs=[VMEM] * 2,
        input_output_aliases={0: 0, 1: 1},
        compiler_params=params(16),
    )(*state, other)


def finish_kernel(tiles, count, *refs):
    qs, stacks, (acc, ml, *outs) = refs[:4], refs[4 : 4 + count], refs[4 + count :]
    keys = [a[0:BLOCK, :] for a in stacks]
    values = [a[BLOCK : 2 * BLOCK, :] for a in stacks]

    def score(t):
        ref, row = tiles[t]
        q = qs[ref][pl.ds(row, CAP), :]
        return [nt(q, k) for k in keys]

    scores = score(0)
    for t in range(CATS):
        ahead = score(t + 1) if t + 1 < CATS else None
        rows = pl.ds(t * CAP, CAP)
        _, l, o = softmax_tile(scores, values, (ml[rows, 0:1], ml[rows, 1:2], acc[rows, :]))
        inverse = 1.0 / l
        mean = jnp.mean(o * o, axis=1, keepdims=True) * inverse * inverse
        outs[t][...] = (o * (inverse * lax.rsqrt(mean + 1e-06))).astype(BF)
        scores = ahead


def finish(qs, tiles, blocks, state):
    return pl.pallas_call(
        functools.partial(finish_kernel, tiles, len(blocks)),
        out_shape=[jax.ShapeDtypeStruct((CAP, D), BF)] * CATS,
        in_specs=[VMEM] * (6 + len(blocks)),
        out_specs=[VMEM] * CATS,
        compiler_params=params(16),
    )(*qs, *blocks, *state)


def collect_kernel(slot_ref, r0, r1, r2, r3, out):
    rows = slot_ref.shape[0]
    slot = jnp.concatenate([slot_ref[...]] * 2, axis=1)
    lane = lax.broadcasted_iota(jnp.int32, (rows, CAP), 1)
    total = None
    for r, ref in enumerate((r0, r1, r2, r3)):
        pick = (lane + r * CAP == slot).astype(BF)
        part = nn(pick, ref[0:CAP, :])
        total = part if total is None else total + part
    out[...] = total.astype(BF)


def collect(slots, returned):
    rows = slots.shape[0]
    return pl.pallas_call(
        collect_kernel,
        out_shape=jax.ShapeDtypeStruct((rows, D), BF),
        in_specs=[VMEM] * 5,
        out_specs=VMEM,
        compiler_params=params(16),
    )(slots, *returned)


def shards(queries, categories, item_keys, item_values):
    rows = queries.shape[0]
    cats = categories.reshape(1, rows)
    here = jnp.concatenate([item_keys, item_values], axis=0)
    far_cats = after(swap_cores(cats), here)
    q0, sent1, sent_far, sent2, far_q0, slots = dispatch(cats, far_cats, queries, swap_cores(queries))
    left, right = first_hop(here, 1), first_hop(here, -1)
    q2 = plane_hop(plane_hop(sent2, 1), 1)
    q1, q3 = plane_hop(sent1, 1), plane_hop(sent_far, 1)
    far_q1, far_q3 = swap_cores(q1), swap_cores(q3)
    far_q2 = swap_cores(after(q2, far_q1, far_q3))
    early = [q0, q1, q3, far_q0, far_q1, far_q3]
    qs = early + [q2, far_q2]
    own = ((0, 0), (1, 0), (5, 0), (6, 0))
    theirs = ((3, 0), (4, 0), (2, 0), (7, 0))
    tiles = own + theirs

    pair = after(jnp.concatenate([left, right], axis=0), slots)
    up_pair, down_pair = second_hop(pair, 1), second_hop(pair, -1)
    far = first_hop(left, 1)
    whole = lambda i, j=0: (i, j, i, j + BLOCK)
    two = 2 * BLOCK

    def same(blocks):
        return ((tuple(blocks), False),) * (2 * CATS)

    first = tuple(whole(i) for i in range(3))
    plan = (((first, True),) * 3 + (((), True),)) * 2
    state = fold(early, tiles, [here, left, right], plan, None, weight=0.3)
    rest = jnp.concatenate([here, after(far, state[0][1])], axis=0)
    up_rest, down_rest = second_hop(rest, 1), second_hop(rest, -1)
    own_far = whole(3)
    plan = (((), False),) * 3 + ((first + (own_far,), True),)
    state = fold(qs, tiles, [here, left, right, far], plan * 2, state, weight=1)
    up_pair, down_pair = after(up_pair, state[0][1]), after(down_pair, state[0][1])
    up_left, down_right = second_hop(up_pair[:two], 1), second_hop(down_pair[two:], -1)
    pair_blocks = tuple(whole(i, j) for i in range(2) for j in (0, two))
    plan = ((pair_blocks + (whole(2),), False),) * 3 + ((pair_blocks, False),)
    state = fold(qs, tiles, [up_pair, down_pair, far], plan * 2, state, weight=1)
    up_here = second_hop(up_rest[:two], 1)
    down_far = second_hop(down_rest[two:], -1)
    mine, others = state
    tail = [up_rest, down_rest, up_left, down_right]
    blocks = tuple([whole(i, j) for i in range(2) for j in (0, two)] + [whole(2), whole(3)])
    todo, skip = (blocks, False), ((), False)
    other = swap_cores(fold(qs, theirs, tail, (todo,) * 4, [others], True, weight=3))
    (mine,) = fold(qs, own, tail, (todo, todo, skip, skip), [mine], weight=3)
    tail = [after(up_rest, up_here, down_far), down_rest, up_left, down_right]
    (mine,) = fold(qs, own, tail, (skip, skip, todo, todo), [mine], weight=3)
    merged = merge(mine, other)
    last = [up_here, down_far]
    last += [swap_cores(a) for a in last]
    mine_q = ((0, 0), (1, 0), (2, 0), (3, 0))
    done = finish([q0, q1, far_q3, q2], mine_q, last, merged)
    back2 = opposite_plane(done[3])
    ahead, behind = plane_hop(done[1], -1), plane_hop(done[2], 1)
    return collect(slots, (done[0], ahead, back2, behind))


def solution(mesh):
    placed = P(("cat", "row", "loop"), None)
    return jax.shard_map(
        shards,
        mesh=mesh,
        in_specs=(placed,) * 4,
        out_specs=placed,
        check_vma=False,
    )
```

```python
import functools
import math

import jax
import jax.numpy as jnp
from jax import lax
from jax.experimental import pallas as pl
from jax.experimental.pallas import tpu as pltpu
from jax.sharding import PartitionSpec as P

D = 512
CAP = 256
CATS = 4
BLOCK = 256
SCALE = 1.4 / math.sqrt(D) * math.log2(math.e)
BF = jnp.bfloat16
F32 = jnp.float32
PLANE = ("row", "loop")
VMEM = pl.BlockSpec(memory_space=pltpu.VMEM)


def place(x, y, core):
    return ((x % 4) * 4 + y % 4) * 2 + core


def hops(first, step):
    pairs = []
    for x in range(4):
        for y in range(4):
            for core in range(2):
                along_x = (core == 0) == first
                to = place(x + step, y, core) if along_x else place(x, y + step, core)
                pairs.append((place(x, y, core), to))
    return pairs


def first_hop(a, step):
    return lax.ppermute(a, PLANE, hops(True, step))


def second_hop(a, step):
    return lax.ppermute(a, PLANE, hops(False, step))


def swap_cores(a):
    return lax.ppermute(a, PLANE, [(i, i ^ 1) for i in range(32)])


def plane_hop(a, step):
    pairs = []
    for cat in range(CATS):
        for i in range(32):
            to = (cat + (step if i % 2 == 0 else -step)) % CATS
            pairs.append((cat * 32 + i, to * 32 + i))
    return lax.ppermute(a, ("cat",) + PLANE, pairs)


def opposite_plane(a):
    return lax.ppermute(a, "cat", [(i, (i + 2) % CATS) for i in range(CATS)])


def after(a, *earlier):
    return lax.optimization_barrier((a, *earlier))[0]


def nt(a, b):
    return lax.dot_general(a, b, (((1,), (1,)), ((), ())), preferred_element_type=F32)


def nn(a, b):
    return jnp.dot(a, b, preferred_element_type=F32)


def params(mib):
    return pltpu.CompilerParams(vmem_limit_bytes=mib * 1024 * 1024)


def classes(cats):
    rows = cats.shape[1]
    ahead = cats - lax.axis_index("cat")
    rel = jnp.where(lax.axis_index("loop") % 2 == 0, ahead, -ahead) & (CATS - 1)
    named = lax.broadcasted_iota(jnp.int32, (16, rows), 0) == rel
    before = lax.broadcasted_iota(jnp.int32, (rows, rows), 0) < lax.broadcasted_iota(
        jnp.int32, (rows, rows), 1
    )
    rank = nn(named.astype(BF), before.astype(BF))
    rank = jnp.sum(jnp.where(named, rank, 0.0), axis=0, keepdims=True)
    return rel * CAP + rank.astype(jnp.int32)


def dispatch_kernel(cat_ref, far_cat_ref, q_ref, far_q_ref, out0, out1, far1, out2, far0, slot_ref):
    rows = cat_ref.shape[1]
    slot, far_slot = classes(cat_ref[...]), classes(far_cat_ref[...])
    iota = lax.broadcasted_iota(jnp.int32, (CAP, rows), 0)

    def pick(r, slots, ref):
        return nn((iota + r * CAP == slots).astype(BF), ref[...]).astype(BF)

    out1[...] = pick(1, slot, q_ref)
    far1[...] = pick(1, far_slot, far_q_ref)
    out2[...] = pick(2, slot, q_ref)
    out0[...] = pick(0, slot, q_ref)
    far0[...] = pick(0, far_slot, far_q_ref)
    column = jnp.transpose(jnp.broadcast_to(slot.astype(F32), (128, rows)))
    slot_ref[...] = column.astype(jnp.int32)


def dispatch(cats, far_cats, queries, far_queries):
    rows = queries.shape[0]
    out = lambda n: jax.ShapeDtypeStruct((n, D), BF)
    return pl.pallas_call(
        dispatch_kernel,
        out_shape=[out(CAP)] * 5
        + [jax.ShapeDtypeStruct((rows, 128), jnp.int32)],
        in_specs=[VMEM] * 4,
        out_specs=[VMEM] * 6,
        compiler_params=params(16),
    )(cats, far_cats, queries, far_queries)


def softmax_tile(scores, values, old):
    m = jnp.max(functools.reduce(jnp.maximum, scores), axis=1, keepdims=True)
    if old is not None:
        m = jnp.maximum(m, old[0])
    es = [jnp.exp2((s - m) * SCALE) for s in scores]
    l = jnp.sum(functools.reduce(jnp.add, es), axis=1, keepdims=True)
    o = functools.reduce(jnp.add, [nn(e.astype(BF), v) for e, v in zip(es, values)])
    if old is not None:
        back = jnp.exp2((old[0] - m) * SCALE)
        l = l + old[1] * back
        o = o + old[2] * back
    return m, l, o


def parts_of(x):
    high = x.astype(BF)
    rest = x - high.astype(F32)
    middle = rest.astype(BF)
    return high, middle, (rest - middle.astype(F32)).astype(BF)


def two_lanes(m, l):
    lane = lax.broadcasted_iota(jnp.int32, (m.shape[0], 128), 1)
    return jnp.where(lane == 0, m, l)


def fold_kernel(plan, tiles, groups, inputs, packed, *refs):
    n_items, n_qs, has_state = inputs
    items, qs, rest = refs[:n_items], refs[n_items : n_items + n_qs], list(refs[n_items + n_qs :])
    states = []
    if has_state:
        states = [(rest.pop(0), rest.pop(0)) for _ in range(groups)]
    outs = rest
    jobs = []
    for i, (blocks, begin) in enumerate(plan):
        group, rows = i // CATS, pl.ds(i % CATS * CAP, CAP)
        if blocks:
            jobs.append((group, i % CATS, tiles[i], blocks, begin))
        elif not begin:
            for ref, out in zip(states[group], outs[2 * group : 2 * group + 2]):
                out[rows, :] = ref[rows, :]

    def score(job):
        ref, row = job[2]
        q = qs[ref][pl.ds(row, CAP), :]
        return [nt(q, items[a][pl.ds(b, BLOCK), :]) for a, b, _, _ in job[3]]

    scores = score(jobs[0])
    for n, (group, t, _, blocks, begin) in enumerate(jobs):
        ahead = score(jobs[n + 1]) if n + 1 < len(jobs) else None
        values = [items[c][pl.ds(d, BLOCK), :] for _, _, c, d in blocks]
        rows = pl.ds(t * CAP, CAP)
        old = None
        if not begin:
            acc, ml = states[group]
            old = (ml[rows, 0:1], ml[rows, 1:2], acc[rows, :])
        m, l, o = softmax_tile(scores, values, old)
        if packed:
            (out,) = outs
            out[rows, 0:D] = (o * (1.0 / l)).astype(BF)
            lane = lax.broadcasted_iota(jnp.int32, (CAP, 128), 1)
            extra = jnp.zeros((CAP, 128), F32)
            for i, part in enumerate(parts_of(m) + parts_of(l)):
                extra = jnp.where(lane == i, part.astype(F32), extra)
            out[rows, D : D + 128] = extra.astype(BF)
        else:
            acc, ml = outs[2 * group : 2 * group + 2]
            acc[rows, :] = o
            ml[rows, :] = two_lanes(m, l)
        scores = ahead


def fold(qs, tiles, items, plan, states, packed=False, weight=1):
    groups = len(tiles) // CATS
    flat = [a for s in states or () for a in s]
    args = [*items, *qs, *flat]
    rows = CATS * CAP
    aliases = {}
    if packed:
        out_shape = [jax.ShapeDtypeStruct((rows, D + 128), BF)]
    else:
        out_shape = [
            jax.ShapeDtypeStruct((rows, D), F32),
            jax.ShapeDtypeStruct((rows, 128), F32),
        ] * groups
        aliases = {len(args) - len(flat) + i: i for i in range(len(flat))}
    work = int(sum(len(blocks) for blocks, _ in plan) * CAP * BLOCK * weight)
    kernel = functools.partial(
        fold_kernel, plan, tiles, groups, (len(items), len(qs), states is not None), packed
    )
    out = pl.pallas_call(
        kernel,
        out_shape=out_shape,
        in_specs=[VMEM] * len(args),
        out_specs=[VMEM] * len(out_shape),
        input_output_aliases=aliases,
        compiler_params=params(24),
        cost_estimate=pl.CostEstimate(
            flops=4 * work * D, bytes_accessed=len(items) * BLOCK * D, transcendentals=work
        ),
    )(*args)
    return out[0] if packed else [tuple(out[2 * g : 2 * g + 2]) for g in range(groups)]


def merge_kernel(acc, ml, other, acc_out, ml_out):
    for t in range(CATS):
        rows = pl.ds(t * CAP, CAP)
        extra = other[rows, D : D + 128].astype(F32)
        m_own, l_own = ml[rows, 0:1], ml[rows, 1:2]
        m_far = extra[:, 0:1] + extra[:, 1:2] + extra[:, 2:3]
        l_far = extra[:, 3:4] + extra[:, 4:5] + extra[:, 5:6]
        m = jnp.maximum(m_own, m_far)
        w_own = jnp.exp2((m_own - m) * SCALE)
        w_far = jnp.exp2((m_far - m) * SCALE) * l_far
        acc_out[rows, :] = acc[rows, :] * w_own + other[rows, 0:D].astype(F32) * w_far
        ml_out[rows, :] = two_lanes(m, l_own * w_own + w_far)


def merge(state, other):
    return pl.pallas_call(
        merge_kernel,
        out_shape=[jax.ShapeDtypeStruct(a.shape, a.dtype) for a in state],
        in_specs=[VMEM] * 3,
        out_specs=[VMEM] * 2,
        input_output_aliases={0: 0, 1: 1},
        compiler_params=params(16),
    )(*state, other)


def finish_kernel(tiles, count, *refs):
    qs, stacks, (acc, ml, *outs) = refs[:4], refs[4 : 4 + count], refs[4 + count :]
    keys = [a[0:BLOCK, :] for a in stacks]
    values = [a[BLOCK : 2 * BLOCK, :] for a in stacks]

    def score(t):
        ref, row = tiles[t]
        q = qs[ref][pl.ds(row, CAP), :]
        return [nt(q, k) for k in keys]

    scores = score(0)
    for t in range(CATS):
        ahead = score(t + 1) if t + 1 < CATS else None
        rows = pl.ds(t * CAP, CAP)
        _, l, o = softmax_tile(scores, values, (ml[rows, 0:1], ml[rows, 1:2], acc[rows, :]))
        inverse = 1.0 / l
        mean = jnp.mean(o * o, axis=1, keepdims=True) * inverse * inverse
        outs[t][...] = (o * (inverse * lax.rsqrt(mean + 1e-06))).astype(BF)
        scores = ahead


def finish(qs, tiles, blocks, state):
    return pl.pallas_call(
        functools.partial(finish_kernel, tiles, len(blocks)),
        out_shape=[jax.ShapeDtypeStruct((CAP, D), BF)] * CATS,
        in_specs=[VMEM] * (6 + len(blocks)),
        out_specs=[VMEM] * CATS,
        compiler_params=params(16),
    )(*qs, *blocks, *state)


def collect_kernel(slot_ref, r0, r1, r2, r3, out):
    rows = slot_ref.shape[0]
    slot = jnp.concatenate([slot_ref[...]] * 2, axis=1)
    lane = lax.broadcasted_iota(jnp.int32, (rows, CAP), 1)
    total = None
    for r, ref in enumerate((r0, r1, r2, r3)):
        pick = (lane + r * CAP == slot).astype(BF)
        part = nn(pick, ref[0:CAP, :])
        total = part if total is None else total + part
    out[...] = total.astype(BF)


def collect(slots, returned):
    rows = slots.shape[0]
    return pl.pallas_call(
        collect_kernel,
        out_shape=jax.ShapeDtypeStruct((rows, D), BF),
        in_specs=[VMEM] * 5,
        out_specs=VMEM,
        compiler_params=params(16),
    )(slots, *returned)


def shards(queries, categories, item_keys, item_values):
    rows = queries.shape[0]
    cats = categories.reshape(1, rows)
    far_cats = swap_cores(cats)
    here = after(jnp.concatenate([item_keys, item_values], axis=0), far_cats)
    q0, sent1, sent_far, sent2, far_q0, slots = dispatch(cats, far_cats, queries, swap_cores(queries))
    left, right = first_hop(here, 1), first_hop(here, -1)
    q2 = plane_hop(plane_hop(sent2, 1), 1)
    q1, q3 = plane_hop(sent1, 1), plane_hop(sent_far, 1)
    far_q1, far_q3 = swap_cores(q1), swap_cores(q3)
    far_q2 = swap_cores(after(q2, far_q1, far_q3))
    early = [q0, q1, q3, far_q0, far_q1, far_q3]
    qs = early + [q2, far_q2]
    own = ((0, 0), (1, 0), (5, 0), (6, 0))
    theirs = ((3, 0), (4, 0), (2, 0), (7, 0))
    tiles = own + theirs

    pair = after(jnp.concatenate([left, right], axis=0), slots)
    up_pair, down_pair = second_hop(pair, 1), second_hop(pair, -1)
    far = first_hop(left, 1)
    whole = lambda i, j=0: (i, j, i, j + BLOCK)
    two = 2 * BLOCK

    def same(blocks):
        return ((tuple(blocks), False),) * (2 * CATS)

    first = tuple(whole(i) for i in range(3))
    plan = (((first, True),) * 3 + (((), True),)) * 2
    state = fold(early, tiles, [here, left, right], plan, None, weight=0.3)
    rest = jnp.concatenate([here, after(far, state[0][1])], axis=0)
    up_rest, down_rest = second_hop(rest, 1), second_hop(rest, -1)
    own_far = whole(3)
    plan = (((), False),) * 3 + ((first + (own_far,), True),)
    state = fold(qs, tiles, [here, left, right, far], plan * 2, state, weight=1)
    up_pair, down_pair = after(up_pair, state[0][1]), after(down_pair, state[0][1])
    up_left, down_right = second_hop(up_pair[:two], 1), second_hop(down_pair[two:], -1)
    pair_blocks = tuple(whole(i, j) for i in range(2) for j in (0, two))
    plan = ((pair_blocks + (whole(2),), False),) * 3 + ((pair_blocks, False),)
    state = fold(qs, tiles, [up_pair, down_pair, far], plan * 2, state, weight=1)
    up_here = second_hop(up_rest[:two], 1)
    down_far = second_hop(down_rest[two:], -1)
    mine, others = state
    tail = [up_rest, down_rest, up_left, down_right]
    blocks = tuple([whole(i, j) for i in range(2) for j in (0, two)] + [whole(2), whole(3)])
    todo, skip = (blocks, False), ((), False)
    other = swap_cores(fold(qs, theirs, tail, (todo,) * 4, [others], True, weight=3))
    (mine,) = fold(qs, own, tail, (todo, todo, skip, skip), [mine], weight=3)
    tail = [after(up_rest, up_here, down_far), down_rest, up_left, down_right]
    (mine,) = fold(qs, own, tail, (skip, skip, todo, todo), [mine], weight=3)
    merged = merge(mine, other)
    last = [up_here, down_far]
    last += [swap_cores(a) for a in last]
    mine_q = ((0, 0), (1, 0), (2, 0), (3, 0))
    done = finish([q0, q1, far_q3, q2], mine_q, last, merged)
    back2 = opposite_plane(done[3])
    ahead, behind = plane_hop(done[1], -1), plane_hop(done[2], 1)
    return collect(slots, (done[0], ahead, back2, behind))


def solution(mesh):
    placed = P(("cat", "row", "loop"), None)
    return jax.shard_map(
        shards,
        mesh=mesh,
        in_specs=(placed,) * 4,
        out_specs=placed,
        check_vma=False,
    )
```
